512 devices in a mesh: row: 16 (over y, core), col: 16 (over z, x_lo), depth: 2 (over x_hi).
Axes of the slice: x: 4 (x_hi: 2, x_lo: 2; x = x_hi * 2 + x_lo), y: 8, z: 8, core: 2. Of those that a mesh axis runs over, the one named last changes fastest.
Arguments:
- tokens: bfloat16 [512, 8192], P(('col', 'depth'), 'row'), may hold values from -6 to 6
- grad_output: bfloat16 [512, 8192], P(('col', 'depth'), 'row'), may hold values from -0.21191406 to 0.21191406
- gate_weight: bfloat16 [8192, 16384], P('row', 'col'), may hold values from -0.0625 to 0.0625
- up_weight: bfloat16 [8192, 16384], P('row', 'col'), may hold values from -0.0625 to 0.0625
- down_weight: bfloat16 [16384, 8192], P('col', 'row'), may hold values from -0.046875 to 0.046875
Outputs:
- input_grad: bfloat16 [512, 8192], P(('col', 'depth'), 'row')
- gate_grad: bfloat16 [8192, 16384], P('row', ('col', 'depth'))
- up_grad: bfloat16 [8192, 16384], P('row', ('col', 'depth'))
- down_grad: bfloat16 [16384, 8192], P(('col', 'depth'), 'row')
The draws below stay inside these ranges and needn't reach their ends.
All inputs are finite; a program needn't handle non-finite values.
Results may differ from the reference program's by a relative error of at most 0.0049.
Values may be sent and summed in bfloat16 or wider, within the bound.
A program may use at most 64 MiB of HBM per device.

```python
import jax
import jax.numpy as jnp

D = 8192
FF = 16384
TOKENS = 512


def level_of(key, extent, split, low, largest):
    level = 1.0
    for position, shards_of in split:
        steps = jax.random.uniform(jax.random.fold_in(jax.random.fold_in(key, 6), position), (shards_of,), jnp.float32, low / len(split), largest / len(split))
        level = level * jnp.repeat(jnp.exp(steps), extent[position] // shards_of).reshape((-1,) + (1,) * (len(extent) - 1 - position))
    return level


def bell_draw(own_key, extent, scale, reach, split=(), kind=jnp.bfloat16):
    values = jax.random.normal(own_key, extent, jnp.float32) * scale
    if len(split) > 0:
        values = level_of(own_key, extent, split, -0.22, 0.18) * values
    return jnp.clip(values, min=-reach, max=reach).astype(kind)


def setup_inputs(seed: int = 0) -> dict:
    key_list = jax.random.split(jax.random.key(seed), 6)
    tokens = bell_draw(key_list[0], (TOKENS, D), 1.0, 6.0, ((0, 32), (1, 16)))
    grad_output = bell_draw(key_list[1], (TOKENS, D), (0.8 * TOKENS ** -0.5), 0.21191406, ((0, 32), (1, 16)))
    gate_weight = bell_draw(key_list[2], (D, FF), D ** -0.5, 0.0625, ((0, 16), (1, 16)))
    up_weight = bell_draw(key_list[3], (D, FF), D ** -0.5, 0.0625, ((0, 16), (1, 16)))
    down_weight = bell_draw(key_list[4], (FF, D), FF ** -0.5, 0.046875, ((0, 16), (1, 16)))
    return {"tokens": tokens, "grad_output": grad_output, "gate_weight": gate_weight, "up_weight": up_weight, "down_weight": down_weight}


def reference(tokens, grad_output, gate_weight, up_weight, down_weight):
    gate_pre = jnp.dot(tokens, gate_weight, preferred_element_type=jnp.float32)
    up_pre = jnp.dot(tokens, up_weight, preferred_element_type=jnp.float32)
    hidden_delta = jnp.dot(grad_output, down_weight.T, preferred_element_type=jnp.float32)
    sigma = jax.nn.sigmoid(gate_pre)
    silu_gate = gate_pre * sigma
    hidden = (silu_gate * up_pre).astype(jnp.bfloat16)
    up_delta = (hidden_delta * silu_gate).astype(jnp.bfloat16)
    slope = sigma * (1.0 + gate_pre * (1.0 - sigma))
    gate_delta = (hidden_delta * up_pre * slope).astype(jnp.bfloat16)
    input_grad = jnp.dot(gate_delta, gate_weight.T, preferred_element_type=jnp.float32)
    input_grad = input_grad + jnp.dot(up_delta, up_weight.T, preferred_element_type=jnp.float32)
    gate_grad = jnp.dot(tokens.T, gate_delta, preferred_element_type=jnp.float32)
    up_grad = jnp.dot(tokens.T, up_delta, preferred_element_type=jnp.float32)
    down_grad = jnp.dot(hidden.T, grad_output, preferred_element_type=jnp.float32)
    return (input_grad.astype(jnp.bfloat16), gate_grad.astype(jnp.bfloat16),
            up_grad.astype(jnp.bfloat16), down_grad.astype(jnp.bfloat16))
```

```python
import functools

import jax
import jax.numpy as jnp
from jax import lax
from jax.experimental import pallas as pl
from jax.experimental.pallas import tpu as pltpu
from jax.sharding import PartitionSpec as P

MESH = pl.DeviceIdType.MESH
OFFSETS = (0, 1, 3, 2)
BACK = (0, 2, 1, 3)
SUM_SCALE = 2.0**48
GRAD_SCALE = 2.0**30


def encode(value, scale):
    scaled = value * scale
    return (scaled * jnp.abs(scaled)).astype(jnp.bfloat16)


def decode(code, scale):
    wide = code.astype(jnp.float32)
    root = jnp.sqrt(jnp.abs(wide)) * (1.0 / scale)
    return jnp.where(wide < 0.0, -root, root)


def dot(left, right, left_dim, right_dim):
    return lax.dot_general(
        left, right, (((left_dim,), (right_dim,)), ((), ())), preferred_element_type=jnp.float32
    )


def kernel(
    ny, nz,
    tok, grd, wg, wu, wd,
    ig_out, gg_out, ug_out, dg_out,
    xg, wgv, wuv, wdv, wgs, wus, wds, pf, sb, rb, hb, own, ib, jb, zf, zs, zr,
    load_sem, az_send, az_recv, ax_send, ax_recv, as_send, as_recv, ws_send, ws_recv,
    b_send, b_recv, c_send, c_recv, cs_send, cs_recv, dx_send, dx_recv, dz_send, dz_recv,
):
    nx = 4
    block, width = tok.shape
    half = wgv.shape[2]
    rows = nz * block
    r, q, d = lax.axis_index("row"), lax.axis_index("col"), lax.axis_index("depth")
    y, k = r // 2, lax.rem(r, 2)
    z, x = q // 2, d * 2 + lax.rem(q, 2)

    def place(py, pz, px, pk):
        return (py * 2 + pk, pz * 2 + lax.rem(px, 2), px // 2)

    def y_peer(step):
        return place(lax.rem(y + step, ny), z, x, k)

    def z_peer(step):
        return place(y, lax.rem(z + step, nz), x, k)

    def x_peer(step):
        return place(y, z, lax.rem(x + step, nx), k)

    sibling = place(y, z, x, 1 - k)

    def remote(src, dst, send, recv, device):
        return pltpu.make_async_remote_copy(
            src_ref=src, dst_ref=dst, send_sem=send, recv_sem=recv, device_id=device, device_id_type=MESH
        )

    loads = [
        pltpu.make_async_copy(tok, xg.at[k, 0, z, 0], load_sem.at[0]),
        pltpu.make_async_copy(grd, xg.at[k, 0, z, 1], load_sem.at[1]),
    ]
    for side in range(2):
        start = pl.multiple_of(d * (2 * half) + side * half, half)
        loads += [
            pltpu.make_async_copy(wg.at[:, pl.ds(start, half)], wgv.at[side], load_sem.at[2 + side]),
            pltpu.make_async_copy(wu.at[:, pl.ds(start, half)], wuv.at[side], load_sem.at[4 + side]),
            pltpu.make_async_copy(wd.at[pl.ds(start, half)], wdv.at[side], load_sem.at[6 + side]),
        ]
    for load in loads:
        load.start()

    barrier = pltpu.get_barrier_semaphore()

    def signal(device):
        pl.semaphore_signal(barrier, inc=1, device_id=device, device_id_type=MESH)

    signal(sibling)
    for step in range(1, nx):
        signal(x_peer(step))
    for step in range(1, nz):
        signal(z_peer(step))
    for step in range(1, ny):
        signal(y_peer(step))
    loads[0].wait()
    loads[1].wait()
    pl.semaphore_wait(barrier, 1 + (nx - 1) + (nz - 1) + (ny - 1))

    def z_copy(step):
        mine = xg.at[k, 0, z]
        return remote(mine, mine, az_send.at[step - 1], az_recv.at[step - 1], z_peer(step))

    def x_copy(chunk, at):
        return remote(
            xg.at[k, 0, at], xg.at[k, BACK[chunk], at],
            ax_send.at[chunk, at], ax_recv.at[BACK[chunk], at], x_peer(OFFSETS[chunk]),
        )

    def twin_copy(chunk):
        ours = xg.at[k, chunk]
        return remote(ours, ours, as_send.at[chunk], as_recv.at[chunk], sibling)

    order = sorted(range(1, nz), key=lambda s: -min(s, nz - s))
    for step in order:
        z_copy(step).start()
    for chunk in range(1, nx):
        x_copy(chunk, z).start()
    for load in loads[2:]:
        load.wait()
    weights = [
        remote(wgv.at[1 - k], wgs, ws_send.at[0], ws_recv.at[0], sibling),
        remote(wuv.at[1 - k], wus, ws_send.at[1], ws_recv.at[1], sibling),
        remote(wdv.at[1 - k], wds, ws_send.at[2], ws_recv.at[2], sibling),
    ]
    for copy in weights:
        copy.start()
    for step in reversed(order):
        z_copy(step).wait_recv()
        at = lax.rem(z + nz - step, nz)
        for chunk in range(1, nx):
            x_copy(chunk, at).start()
    twin_copy(0).start()
    for copy in weights:
        copy.wait_recv()

    def b_copy(chunk, step):
        return remote(
            sb.at[chunk, lax.rem(y + step, ny)], rb.at[chunk, step - 1],
            b_send.at[chunk, step - 1], b_recv.at[chunk, step - 1], y_peer(step),
        )

    y_order = sorted(range(1, ny), key=lambda s: -min(s, ny - s))
    for chunk in range(nx):
        if chunk > 0:
            for at in range(nz):
                x_copy(BACK[chunk], at).wait_recv()
            twin_copy(chunk).start()
        ours = xg[k, chunk]
        left = ours[:, 0].reshape(rows, width)
        left_grad = ours[:, 1].reshape(rows, width)
        sums = [
            dot(left, wgv[k], 1, 0),
            dot(left, wuv[k], 1, 0),
            dot(left_grad, wdv[k], 1, 1),
        ]
        twin_copy(chunk).wait_recv()
        other = xg[1 - k, chunk]
        right = other[:, 0].reshape(rows, width)
        right_grad = other[:, 1].reshape(rows, width)
        sums[0] += dot(right, wgs[...], 1, 0)
        sums[1] += dot(right, wus[...], 1, 0)
        sums[2] += dot(right_grad, wds[...], 1, 1)
        for part in range(3):
            cols = pl.ds(part * half, half)
            pf[chunk, :, :, cols] = sums[part].reshape(ny, block, half)
            sb[chunk, :, :, cols] = encode(sums[part], SUM_SCALE).reshape(ny, block, half)
        for step in y_order:
            b_copy(chunk, step).start()

    def c_copy(chunk, step):
        mine = hb.at[chunk, k, y]
        return remote(mine, mine, c_send.at[chunk, step - 1], c_recv.at[chunk, step - 1], y_peer(step))

    def half_copy(chunk):
        ours = hb.at[chunk, k]
        return remote(ours, ours, cs_send.at[chunk], cs_recv.at[chunk], sibling)

    for chunk in range(nx):
        for step in range(1, ny):
            b_copy(chunk, step).wait_recv()
        total = pf[chunk, y]
        for step in range(1, ny):
            total += decode(rb[chunk, step - 1], SUM_SCALE)
        gate_pre = total[:, :half]
        up_pre = total[:, half : 2 * half]
        hidden_delta = total[:, 2 * half :]
        sigma = jax.nn.sigmoid(gate_pre)
        silu_gate = gate_pre * sigma
        slope = sigma * (1.0 + gate_pre * (1.0 - sigma))
        hb[chunk, k, y, 0] = (silu_gate * up_pre).astype(jnp.bfloat16)
        hb[chunk, k, y, 1] = (hidden_delta * up_pre * slope).astype(jnp.bfloat16)
        hb[chunk, k, y, 2] = (hidden_delta * silu_gate).astype(jnp.bfloat16)
        for step in y_order:
            c_copy(chunk, step).start()

    def dx_copy(chunk):
        return remote(
            ib.at[chunk], jb.at[BACK[chunk]], dx_send.at[chunk], dx_recv.at[BACK[chunk]], x_peer(OFFSETS[chunk])
        )

    def term(chunk, side):
        gate = hb[chunk, side, :, 1].reshape(rows, half)
        up = hb[chunk, side, :, 2].reshape(rows, half)
        return dot(gate, wgv[side], 1, 1) + dot(up, wuv[side], 1, 1)

    for chunk in (1, 2, 3, 0):
        for step in range(1, ny):
            c_copy(chunk, step).wait_recv()
        half_copy(chunk).start()
        total = term(chunk, k)
        half_copy(chunk).wait_recv()
        total = (total + term(chunk, 1 - k)).reshape(nz, block, width)
        if chunk == 0:
            own[...] = total
        else:
            ib[chunk] = encode(total, GRAD_SCALE)
            dx_copy(chunk).start()

    tokens = nx * rows

    def gradient(out, of_tokens, part):
        left = xg[k, :, :, of_tokens].reshape(tokens, width)
        for side in range(2):
            right = hb[:, side, :, part].reshape(tokens, half)
            out[:, pl.ds(side * half, half)] = dot(left, right, 0, 0).astype(jnp.bfloat16)

    gradient(gg_out, 0, 1)
    for chunk in range(1, nx):
        dx_copy(BACK[chunk]).wait_recv()
    total = own[...]
    for chunk in range(1, nx):
        total += decode(jb[chunk], GRAD_SCALE)
    zf[...] = total
    zs[...] = encode(total, GRAD_SCALE)

    def dz_copy(step):
        return remote(
            zs.at[lax.rem(z + step, nz)], zr.at[step - 1], dz_send.at[step - 1], dz_recv.at[step - 1], z_peer(step)
        )

    for step in order:
        dz_copy(step).start()
    gradient(ug_out, 0, 2)
    right = xg[k, :, :, 1].reshape(tokens, width)
    for side in range(2):
        left = hb[:, side, :, 0].reshape(tokens, half)
        dg_out[pl.ds(side * half, half)] = dot(left, right, 0, 0).astype(jnp.bfloat16)
    for step in range(1, nz):
        dz_copy(step).wait_recv()
    total = zf[z]
    for step in range(1, nz):
        total += decode(zr[step - 1], GRAD_SCALE)
    ig_out[...] = total.astype(jnp.bfloat16)

    for copy in weights:
        copy.wait_send()
    for step in range(1, nz):
        z_copy(step).wait_send()
        dz_copy(step).wait_send()
    for chunk in range(1, nx):
        for at in range(nz):
            x_copy(chunk, at).wait_send()
        dx_copy(chunk).wait_send()
    for chunk in range(nx):
        twin_copy(chunk).wait_send()
        half_copy(chunk).wait_send()
        for step in range(1, ny):
            b_copy(chunk, step).wait_send()
            c_copy(chunk, step).wait_send()


def shards(ny, nz, tokens, grad_output, gate_weight, up_weight, down_weight):
    block, width = tokens.shape
    hidden = gate_weight.shape[1] // 2
    half = hidden // 2
    nx = 4
    bf16, f32 = jnp.bfloat16, jnp.float32
    vmem, dma = pltpu.VMEM, pltpu.SemaphoreType.DMA
    return pl.pallas_call(
        functools.partial(kernel, ny, nz),
        out_shape=(
            jax.ShapeDtypeStruct((block, width), bf16),
            jax.ShapeDtypeStruct((width, hidden), bf16),
            jax.ShapeDtypeStruct((width, hidden), bf16),
            jax.ShapeDtypeStruct((hidden, width), bf16),
        ),
        in_specs=[pl.BlockSpec(memory_space=pl.ANY)] * 5,
        out_specs=[pl.BlockSpec(memory_space=vmem)] * 4,
        scratch_shapes=[
            vmem((2, nx, nz, 2, block, width), bf16),
            vmem((2, width, half), bf16),
            vmem((2, width, half), bf16),
            vmem((2, half, width), bf16),
            vmem((width, half), bf16),
            vmem((width, half), bf16),
            vmem((half, width), bf16),
            vmem((nx, ny, block, 3 * half), f32),
            vmem((nx, ny, block, 3 * half), bf16),
            vmem((nx, ny - 1, block, 3 * half), bf16),
            vmem((nx, 2, ny, 3, block, half), bf16),
            vmem((nz, block, width), f32),
            vmem((nx, nz, block, width), bf16),
            vmem((nx, nz, block, width), bf16),
            vmem((nz, block, width), f32),
            vmem((nz, block, width), bf16),
            vmem((nz - 1, block, width), bf16),
            dma((8,)),
            dma((nz - 1,)), dma((nz - 1,)),
            dma((nx, nz)), dma((nx, nz)),
            dma((nx,)), dma((nx,)),
            dma((3,)), dma((3,)),
            dma((nx, ny - 1)), dma((nx, ny - 1)),
            dma((nx, ny - 1)), dma((nx, ny - 1)),
            dma((nx,)), dma((nx,)),
            dma((nx,)), dma((nx,)),
            dma((nz - 1,)), dma((nz - 1,)),
        ],
        compiler_params=pltpu.CompilerParams(
            collective_id=0, has_side_effects=True, vmem_limit_bytes=60 * 2**20
        ),
        name="ffn_backward",
    )(tokens, grad_output, gate_weight, up_weight, down_weight)


def solution(mesh):
    placed = (
        P(("col", "depth"), "row"),
        P(("col", "depth"), "row"),
        P("row", "col"),
        P("row", "col"),
        P("col", "row"),
    )
    ny, nz = mesh.shape["row"] // 2, mesh.shape["col"] // 2
    return jax.shard_map(
        functools.partial(shards, ny, nz),
        mesh=mesh,
        in_specs=placed,
        out_specs=(
            P(("col", "depth"), "row"),
            P("row", ("col", "depth")),
            P("row", ("col", "depth")),
            P(("col", "depth"), "row"),
        ),
        check_vma=False,
    )
```

```python
import functools

import jax
import jax.numpy as jnp
from jax import lax
from jax.experimental import pallas as pl
from jax.experimental.pallas import tpu as pltpu
from jax.sharding import PartitionSpec as P

MESH = pl.DeviceIdType.MESH
OFFSETS = (0, 1, 3, 2)
BACK = (0, 2, 1, 3)
SUM_SCALE = 2.0**48
GRAD_SCALE = 2.0**30


def encode(value, scale):
    scaled = value * scale
    return (scaled * jnp.abs(scaled)).astype(jnp.bfloat16)


def decode(code, scale):
    wide = code.astype(jnp.float32)
    root = jnp.sqrt(jnp.abs(wide)) * (1.0 / scale)
    return jnp.where(wide < 0.0, -root, root)


def dot(left, right, left_dim, right_dim):
    return lax.dot_general(
        left, right, (((left_dim,), (right_dim,)), ((), ())), preferred_element_type=jnp.float32
    )


STEPS = (
    ("sum", 0), ("fetch", 3), ("fetch", 1), ("sum", 3), ("fetch", 2), ("sum", 1), ("sum", 2),
    ("join", 0), ("join", 3), ("join", 1), ("join", 2), ("gate", 3), ("gate", 1), ("gate", 2), ("gate", 0),
    ("pass", 3), ("pass", 1), ("pass", 2), ("pass", 0),
    ("half", 3), ("half", 1), ("grad", 3), ("half", 2), ("grad", 1), ("half", 0), ("grad", 2), ("grad", 0),
)


def kernel(
    ny, nz,
    tok, grd, wg, wu, wd,
    ig_out, gg_out, ug_out, dg_out,
    xg, wgv, wuv, wdv, wgs, wus, wds, pf, sb, pa, pb, pc, sc, rc, hb, own, ib, jb, zf, zs, zr, ggv, ugv, dgv, igv,
    load_sem, az_send, az_recv, ax_send, ax_recv, as_send, as_recv, ws_send, ws_recv,
    b_send, b_recv, c_send, c_recv, cs_send, cs_recv, dx_send, dx_recv, dz_send, dz_recv,
):
    nx = 4
    block, width = tok.shape
    half = wgv.shape[2]
    rows = nz * block
    r, q, d = lax.axis_index("row"), lax.axis_index("col"), lax.axis_index("depth")
    y, k = r // 2, lax.rem(r, 2)
    z, x = q // 2, d * 2 + lax.rem(q, 2)

    def place(py, pz, px, pk):
        return (py * 2 + pk, pz * 2 + lax.rem(px, 2), px // 2)

    def along_y(step):
        return lax.rem(y + step + ny, ny)

    def along_z(step):
        return lax.rem(z + step + nz, nz)

    def y_peer(step):
        return place(along_y(step), z, x, k)

    def z_peer(step):
        return place(y, along_z(step), x, k)

    def x_peer(step):
        return place(y, z, lax.rem(x + step, nx), k)

    sibling = place(y, z, x, 1 - k)
    far = 2 - 4 * k
    sent = []

    def remote(src, dst, send, recv, device):
        return pltpu.make_async_remote_copy(
            src_ref=src, dst_ref=dst, send_sem=send, recv_sem=recv, device_id=device, device_id_type=MESH
        )

    def start(copy):
        copy.start()
        sent.append(copy)

    loads = [
        pltpu.make_async_copy(tok, xg.at[k, 0, z, 0], load_sem.at[0]),
        pltpu.make_async_copy(grd, xg.at[k, 0, z, 1], load_sem.at[1]),
    ]
    for side in range(2):
        first = pl.multiple_of(d * (2 * half) + side * half, half)
        loads += [
            pltpu.make_async_copy(wg.at[:, pl.ds(first, half)], wgv.at[side], load_sem.at[2 + side]),
            pltpu.make_async_copy(wu.at[:, pl.ds(first, half)], wuv.at[side], load_sem.at[4 + side]),
            pltpu.make_async_copy(wd.at[pl.ds(first, half)], wdv.at[side], load_sem.at[6 + side]),
        ]
    for load in loads:
        load.start()

    barrier = pltpu.get_barrier_semaphore()
    friends = [sibling]
    friends += [z_peer(step) for step in range(1, nz)]
    friends += [x_peer(step) for step in range(1, nx)]
    friends += [y_peer(step) for step in (1, -1, 2, -2)]
    for device in friends:
        pl.semaphore_signal(barrier, inc=1, device_id=device, device_id_type=MESH)
    loads[0].wait()
    loads[1].wait()
    pl.semaphore_wait(barrier, len(friends))

    def ring_copy(buffer, at, peer, send, recv, origin, number, target):
        piece = buffer.at[at(origin)]
        return remote(piece, piece, send.at[number], recv.at[number], peer(target))

    def ring_first(ring):
        for target in (2, -2, 1, -1):
            start(ring_copy(*ring, 0, target % 8, target))

    def ring_second(ring):
        ring_wait(ring, 2)
        ring_wait(ring, 6)
        start(ring_copy(*ring, -far, 4, far))
        start(ring_copy(*ring, -2, 3, 1))
        start(ring_copy(*ring, 2, 5, -1))

    def ring_wait(ring, number):
        ring_copy(*ring, -number, number, 0).wait_recv()

    z_ring = (xg.at[k, 0], along_z, z_peer, az_send.at[0], az_recv.at[0])
    far_ring = (xg.at[k, 3], along_z, z_peer, az_send.at[1], az_recv.at[1])

    def x_copy(chunk, at):
        return remote(
            xg.at[k, 0, at], xg.at[k, BACK[chunk], at],
            ax_send.at[chunk, at], ax_recv.at[BACK[chunk], at], x_peer(OFFSETS[chunk]),
        )

    def twin_copy(chunk):
        ours = xg.at[k, chunk]
        return remote(ours, ours, as_send.at[chunk], as_recv.at[chunk], sibling)

    def spread(number):
        for chunk in (1, 2):
            start(x_copy(chunk, along_z(-number)))

    start(x_copy(3, z))
    ring_first(z_ring)
    spread(0)
    for load in loads[2:]:
        load.wait()
    weights = [
        remote(wgv.at[1 - k], wgs, ws_send.at[0], ws_recv.at[0], sibling),
        remote(wuv.at[1 - k], wus, ws_send.at[1], ws_recv.at[1], sibling),
        remote(wdv.at[1 - k], wds, ws_send.at[2], ws_recv.at[2], sibling),
    ]
    for copy in weights:
        start(copy)
    for number in (1, 7):
        ring_wait(z_ring, number)
        spread(number)
    x_copy(3, z).wait_recv()
    ring_first(far_ring)
    ring_second(z_ring)
    for number in (2, 6):
        spread(number)
    for number in (3, 5, 4):
        ring_wait(z_ring, number)
        spread(number)
    start(twin_copy(0))
    ring_second(far_ring)
    for copy in weights:
        copy.wait_recv()

    def fetch(chunk):
        if chunk == 3:
            for number in (1, 7, 3, 5, 4):
                ring_wait(far_ring, number)
        else:
            for at in range(nz):
                x_copy(BACK[chunk], at).wait_recv()
        start(twin_copy(chunk))

    def pair_copy(chunk, side):
        return remote(
            sb.at[chunk, pl.ds(2 * side, 2)], (pa, pb)[side].at[chunk],
            b_send.at[chunk, side], b_recv.at[chunk, side], y_peer((1, -1)[side]),
        )

    def far_copy(chunk):
        return remote(sb.at[chunk, 4], pc.at[chunk], b_send.at[chunk, 2], b_recv.at[chunk, 2], y_peer(-far))

    def join_copy(chunk, side):
        return remote(
            sc.at[chunk, side], rc.at[chunk, side],
            b_send.at[chunk, 3 + side], b_recv.at[chunk, 3 + side], y_peer((2, -2)[side]),
        )

    def add_features(chunk):
        ours = xg[k, chunk]
        left = ours[:, 0].reshape(rows, width)
        left_grad = ours[:, 1].reshape(rows, width)
        sums = [
            dot(left, wgv[k], 1, 0),
            dot(left, wuv[k], 1, 0),
            dot(left_grad, wdv[k], 1, 1),
        ]
        twin_copy(chunk).wait_recv()
        other = xg[1 - k, chunk]
        right = other[:, 0].reshape(rows, width)
        right_grad = other[:, 1].reshape(rows, width)
        sums[0] += dot(right, wgs[...], 1, 0)
        sums[1] += dot(right, wus[...], 1, 0)
        sums[2] += dot(right_grad, wds[...], 1, 1)
        for part in range(3):
            pf[chunk, :, :, pl.ds(part * half, half)] = sums[part].reshape(ny, block, half)
        for slot, step in enumerate((1, 3, -1, -3, 4)):
            sb[chunk, slot] = encode(pf[chunk, along_y(step)], SUM_SCALE)
        start(far_copy(chunk))
        start(pair_copy(chunk, 0))
        start(pair_copy(chunk, 1))

    def join(chunk):
        pair_copy(chunk, 0).wait_recv()
        pair_copy(chunk, 1).wait_recv()
        far_copy(chunk).wait_recv()
        distant = decode(pc[chunk], SUM_SCALE)
        share = k.astype(jnp.float32)
        ahead = pf[chunk, along_y(2)] + decode(pa[chunk, 1], SUM_SCALE) + distant * share
        behind = pf[chunk, along_y(-2)] + decode(pb[chunk, 1], SUM_SCALE) + distant * (1.0 - share)
        sc[chunk, 0] = encode(ahead, SUM_SCALE)
        sc[chunk, 1] = encode(behind, SUM_SCALE)
        start(join_copy(chunk, 0))
        start(join_copy(chunk, 1))

    def y_ring(chunk):
        return (hb.at[chunk, k], along_y, y_peer, c_send.at[chunk], c_recv.at[chunk])

    def half_copy(chunk):
        ours = hb.at[chunk, k]
        return remote(ours, ours, cs_send.at[chunk], cs_recv.at[chunk], sibling)

    def gate(chunk):
        join_copy(chunk, 0).wait_recv()
        join_copy(chunk, 1).wait_recv()
        total = pf[chunk, y] + decode(pa[chunk, 0], SUM_SCALE) + decode(pb[chunk, 0], SUM_SCALE)
        total += decode(rc[chunk, 0], SUM_SCALE) + decode(rc[chunk, 1], SUM_SCALE)
        gate_pre = total[:, :half]
        up_pre = total[:, half : 2 * half]
        hidden_delta = total[:, 2 * half :]
        sigma = jax.nn.sigmoid(gate_pre)
        silu_gate = gate_pre * sigma
        slope = sigma * (1.0 + gate_pre * (1.0 - sigma))
        hb[chunk, k, y, 0] = (silu_gate * up_pre).astype(jnp.bfloat16)
        hb[chunk, k, y, 1] = (hidden_delta * up_pre * slope).astype(jnp.bfloat16)
        hb[chunk, k, y, 2] = (hidden_delta * silu_gate).astype(jnp.bfloat16)
        ring_first(y_ring(chunk))

    def dx_copy(chunk):
        return remote(
            ib.at[chunk], jb.at[BACK[chunk]], dx_send.at[chunk], dx_recv.at[BACK[chunk]], x_peer(OFFSETS[chunk])
        )

    def term(chunk, side):
        gate_delta = hb[chunk, side, :, 1].reshape(rows, half)
        up_delta = hb[chunk, side, :, 2].reshape(rows, half)
        return dot(gate_delta, wgv[side], 1, 1) + dot(up_delta, wuv[side], 1, 1)

    def share_half(chunk):
        for number in (1, 7, 3, 5, 4):
            ring_wait(y_ring(chunk), number)
        start(half_copy(chunk))

    def grad(chunk):
        total = term(chunk, k)
        half_copy(chunk).wait_recv()
        total = (total + term(chunk, 1 - k)).reshape(nz, block, width)
        if chunk == 0:
            own[...] = total
        else:
            ib[chunk] = encode(total, GRAD_SCALE)
            start(dx_copy(chunk))

    actions = {
        "fetch": fetch, "sum": add_features, "join": join, "gate": gate,
        "pass": lambda chunk: ring_second(y_ring(chunk)), "half": share_half, "grad": grad,
    }
    for name, chunk in STEPS:
        actions[name](chunk)

    for chunk in range(1, nx):
        dx_copy(BACK[chunk]).wait_recv()
    total = own[...]
    for chunk in range(1, nx):
        total += decode(jb[chunk], GRAD_SCALE)
    zf[...] = total
    zs[...] = encode(total, GRAD_SCALE)

    def dz_copy(step):
        return remote(zs.at[along_z(step)], zr.at[step - 1], dz_send.at[step - 1], dz_recv.at[step - 1], z_peer(step))

    for step in (4, 3, 5, 2, 6, 1, 7):
        start(dz_copy(step))

    tokens = nx * rows
    left = xg[k, :, :, 0].reshape(tokens, width)
    for side in range(2):
        cols = pl.ds(side * half, half)
        ggv[:, cols] = dot(left, hb[:, side, :, 1].reshape(tokens, half), 0, 0).astype(jnp.bfloat16)
        ugv[:, cols] = dot(left, hb[:, side, :, 2].reshape(tokens, half), 0, 0).astype(jnp.bfloat16)
    stores = [
        pltpu.make_async_copy(ggv, gg_out, load_sem.at[0]),
        pltpu.make_async_copy(ugv, ug_out, load_sem.at[1]),
        pltpu.make_async_copy(dgv, dg_out, load_sem.at[2]),
        pltpu.make_async_copy(igv, ig_out, load_sem.at[3]),
    ]
    stores[0].start()
    stores[1].start()
    right = xg[k, :, :, 1].reshape(tokens, width)
    for side in range(2):
        cols = pl.ds(side * half, half)
        dgv[cols] = dot(hb[:, side, :, 0].reshape(tokens, half), right, 0, 0).astype(jnp.bfloat16)
    stores[2].start()

    for step in range(1, nz):
        dz_copy(step).wait_recv()
    total = zf[z]
    for step in range(1, nz):
        total += decode(zr[step - 1], GRAD_SCALE)
    igv[...] = total.astype(jnp.bfloat16)
    stores[3].start()

    for copy in sent:
        copy.wait_send()
    for store in stores:
        store.wait()


def hand_over(*refs):
    count = len(refs) // 3
    given, out, held, sems = refs[:count], refs[count : 2 * count], refs[2 * count : 3 * count], refs[-1]
    loads = [pltpu.make_async_copy(given[i], held[i], sems.at[0, i]) for i in range(count)]
    stores = [pltpu.make_async_copy(held[i], out[i], sems.at[1, i]) for i in range(count)]
    for load in loads:
        load.start()
    for load, store in zip(loads, stores):
        load.wait()
        store.start()
    for store in stores:
        store.wait()


def shards(ny, nz, tokens, grad_output, gate_weight, up_weight, down_weight):
    block, width = tokens.shape
    hidden = gate_weight.shape[1] // 2
    half = hidden // 2
    nx = 4
    bf16, f32 = jnp.bfloat16, jnp.float32
    vmem, dma = pltpu.VMEM, pltpu.SemaphoreType.DMA
    results = (
        jax.ShapeDtypeStruct((block, width), bf16),
        jax.ShapeDtypeStruct((width, hidden), bf16),
        jax.ShapeDtypeStruct((width, hidden), bf16),
        jax.ShapeDtypeStruct((hidden, width), bf16),
    )
    made = pl.pallas_call(
        functools.partial(kernel, ny, nz),
        out_shape=results,
        in_specs=[pl.BlockSpec(memory_space=pl.ANY)] * 5,
        out_specs=[pl.BlockSpec(memory_space=pl.ANY)] * 4,
        scratch_shapes=[
            vmem((2, nx, nz, 2, block, width), bf16),
            vmem((2, width, half), bf16),
            vmem((2, width, half), bf16),
            vmem((2, half, width), bf16),
            vmem((width, half), bf16),
            vmem((width, half), bf16),
            vmem((half, width), bf16),
            vmem((nx, ny, block, 3 * half), f32),
            vmem((nx, 5, block, 3 * half), bf16),
            vmem((nx, 2, block, 3 * half), bf16),
            vmem((nx, 2, block, 3 * half), bf16),
            vmem((nx, block, 3 * half), bf16),
            vmem((nx, 2, block, 3 * half), bf16),
            vmem((nx, 2, block, 3 * half), bf16),
            vmem((nx, 2, ny, 3, block, half), bf16),
            vmem((nz, block, width), f32),
            vmem((nx, nz, block, width), bf16),
            vmem((nx, nz, block, width), bf16),
            vmem((nz, block, width), f32),
            vmem((nz, block, width), bf16),
            vmem((nz - 1, block, width), bf16),
            vmem((width, hidden), bf16),
            vmem((width, hidden), bf16),
            vmem((hidden, width), bf16),
            vmem((block, width), bf16),
            dma((8,)),
            dma((2, nz)), dma((2, nz)),
            dma((nx, nz)), dma((nx, nz)),
            dma((nx,)), dma((nx,)),
            dma((3,)), dma((3,)),
            dma((nx, 5)), dma((nx, 5)),
            dma((nx, ny)), dma((nx, ny)),
            dma((nx,)), dma((nx,)),
            dma((nx,)), dma((nx,)),
            dma((nz - 1,)), dma((nz - 1,)),
        ],
        compiler_params=pltpu.CompilerParams(
            collective_id=0, has_side_effects=True, vmem_limit_bytes=60 * 2**20
        ),
        name="ffn_backward",
    )(tokens, grad_output, gate_weight, up_weight, down_weight)
    return pl.pallas_call(
        hand_over,
        out_shape=results,
        in_specs=[pl.BlockSpec(memory_space=pl.ANY)] * 4,
        out_specs=[pl.BlockSpec(memory_space=pl.ANY)] * 4,
        scratch_shapes=[vmem(result.shape, bf16) for result in results] + [dma((2, 4))],
        compiler_params=pltpu.CompilerParams(vmem_limit_bytes=60 * 2**20),
        name="hand_over",
    )(*made)


def solution(mesh):
    placed = (
        P(("col", "depth"), "row"),
        P(("col", "depth"), "row"),
        P("row", "col"),
        P("row", "col"),
        P("col", "row"),
    )
    ny, nz = mesh.shape["row"] // 2, mesh.shape["col"] // 2
    return jax.shard_map(
        functools.partial(shards, ny, nz),
        mesh=mesh,
        in_specs=placed,
        out_specs=(
            P(("col", "depth"), "row"),
            P("row", ("col", "depth")),
            P("row", ("col", "depth")),
            P(("col", "depth"), "row"),
        ),
        check_vma=False,
    )
```

```python
import functools

import jax
import jax.numpy as jnp
from jax import lax
from jax.experimental import pallas as pl
from jax.experimental.pallas import tpu as pltpu
from jax.sharding import PartitionSpec as P

MESH = pl.DeviceIdType.MESH
OFFSETS = (0, 1, 3, 2)
BACK = (0, 2, 1, 3)
SLOTS = (0, 1, -1, 2, -2, 3, -3, 4)
SUM_SCALE = 2.0**48
GRAD_SCALE = 2.0**30


def encode(value, scale):
    scaled = value * scale
    return (scaled * jnp.abs(scaled)).astype(jnp.bfloat16)


def decode(code, scale):
    wide = code.astype(jnp.float32)
    root = jnp.sqrt(jnp.abs(wide)) * (1.0 / scale)
    return jnp.where(wide < 0.0, -root, root)


def dot(left, right, left_dim, right_dim):
    return lax.dot_general(
        left, right, (((left_dim,), (right_dim,)), ((), ())), preferred_element_type=jnp.float32
    )


STEPS = (
    "near0", "fetch0", "sum0", "fetch2", "fetch4", "far0", "rest0", "sum2", "sum4", "fetch6", "fetch1", "join0",
    "sum6", "sum1", "join2", "join4", "fetch3", "fetch5", "fetch7", "gate0", "join6", "sum3", "sum5", "sum7",
    "join1", "gate2", "gate4", "pass0", "join3", "join5", "join7", "gate6", "pass2", "pass4", "gate3", "half0",
    "pass6", "gate5", "gate7", "gate1", "grad0", "half2", "half4", "grad2", "pass3", "grad4", "half6", "pass5",
    "pass7", "pass1", "grad6", "half3", "half5", "grad3", "half7", "grad5", "half1", "grad7", "grad1", "merge1",
)


def kernel(
    ny, nz,
    tok, grd, wg, wu, wd,
    ig_out, gg_out, ug_out, dg_out,
    xg, wgv, wuv, wdv, wgs, wus, wds, xo, pf, sb, pa, pb, pc, sc, rc, hb, ho, own, ib, jb, mb, tail, ggv, ugv, dgv, igv,
    load_sem, az_send, az_recv, ax_send, ax_recv, as_send, as_recv, ws_send, ws_recv,
    b_send, b_recv, c_send, c_recv, cs_send, cs_recv, dx_send, dx_recv, mx_send, mx_recv,
):
    nx = 4
    block, width = tok.shape
    half = wgv.shape[2]
    blocks = nz // 2
    rows = blocks * block
    share = rows // ny
    cut = half // 2
    r, q, d = lax.axis_index("row"), lax.axis_index("col"), lax.axis_index("depth")
    y, k = r // 2, lax.rem(r, 2)
    z, x = q // 2, d * 2 + lax.rem(q, 2)

    def place(py, pz, px, pk):
        return (py * 2 + pk, pz * 2 + lax.rem(px, 2), px // 2)

    def along_y(step):
        return lax.rem(y + step + ny, ny)

    def along_z(step):
        return lax.rem(z + step + nz, nz)

    def y_peer(step):
        return place(along_y(step), z, x, k)

    def plane_peer(step, across):
        return place(y, along_z(step), lax.rem(x + across, nx), k)

    def z_peer(step):
        return plane_peer(step, 0)

    def x_peer(across):
        return plane_peer(0, across)

    sibling = place(y, z, x, 1 - k)
    far = 2 - 4 * k
    sent = []

    def remote(src, dst, send, recv, device):
        return pltpu.make_async_remote_copy(
            src_ref=src, dst_ref=dst, send_sem=send, recv_sem=recv, device_id=device, device_id_type=MESH
        )

    def start(copy):
        copy.start()
        sent.append(copy)

    loads = [
        pltpu.make_async_copy(tok, xg.at[k, 0, 0, 0], load_sem.at[0]),
        pltpu.make_async_copy(grd, xg.at[k, 0, 0, 1], load_sem.at[1]),
    ]
    for side in range(2):
        first = pl.multiple_of(d * (2 * half) + side * half, half)
        loads += [
            pltpu.make_async_copy(wg.at[:, pl.ds(first, half)], wgv.at[side], load_sem.at[2 + side]),
            pltpu.make_async_copy(wu.at[:, pl.ds(first, half)], wuv.at[side], load_sem.at[4 + side]),
            pltpu.make_async_copy(wd.at[pl.ds(first, half)], wdv.at[side], load_sem.at[6 + side]),
        ]
    for load in loads:
        load.start()

    barrier = pltpu.get_barrier_semaphore()
    friends = [sibling]
    friends += [z_peer(step) for step in (1, -1, 2, -2)]
    friends += [x_peer(across) for across in range(1, nx)]
    friends += [y_peer(step) for step in (1, -1, 2, -2)]
    for device in friends:
        pl.semaphore_signal(barrier, inc=1, device_id=device, device_id_type=MESH)
    loads[0].wait()
    loads[1].wait()
    pl.semaphore_wait(barrier, len(friends))

    def ring_copy(ring, origin, number, target):
        buffer, mine, theirs, peer, send, recv = ring
        return remote(
            buffer.at[mine(origin)], buffer.at[theirs(origin, number)], send.at[number], recv.at[number], peer(target)
        )

    def ring_first(ring):
        for target in (2, -2, 1, -1):
            start(ring_copy(ring, 0, target % 8, target))

    def ring_second(ring):
        ring_wait(ring, 2)
        ring_wait(ring, 6)
        start(ring_copy(ring, None, 4, far))
        start(ring_copy(ring, -2, 3, 1))
        start(ring_copy(ring, 2, 5, -1))

    def ring_wait(ring, number):
        buffer, mine, theirs, peer, send, recv = ring
        place_of = buffer.at[theirs(-number, number)]
        remote(place_of, place_of, send.at[number], recv.at[number], peer(1)).wait_recv()

    def slot(origin):
        return SLOTS.index((origin + 3) % 8 - 3)

    def z_mine(origin):
        return slot(2) * k + slot(-2) * (1 - k) if origin is None else slot(origin)

    def z_ring(column, which):
        return (
            xg.at[k, column], z_mine, lambda origin, number: slot(-number), z_peer, az_send.at[which], az_recv.at[which]
        )

    own_ring, far_ring = z_ring(0, 0), z_ring(3, 1)

    def x_copy(column, at):
        return remote(
            xg.at[k, 0, at], xg.at[k, BACK[column], at],
            ax_send.at[column, at], ax_recv.at[BACK[column], at], x_peer(OFFSETS[column]),
        )

    def twin_copy(chunk):
        ours = xg.at[k, chunk // 2, pl.ds(chunk % 2 * blocks, blocks)]
        return remote(ours, ours, as_send.at[chunk], as_recv.at[chunk], sibling)

    def spread(origin):
        for column in (1, 2):
            start(x_copy(column, slot(origin)))

    start(x_copy(3, 0))
    ring_first(own_ring)
    spread(0)
    for load in loads[2:]:
        load.wait()
    weights = [
        remote(wgv.at[1 - k], wgs, ws_send.at[0], ws_recv.at[0], sibling),
        remote(wuv.at[1 - k], wus, ws_send.at[1], ws_recv.at[1], sibling),
        remote(wdv.at[1 - k], wds, ws_send.at[2], ws_recv.at[2], sibling),
    ]
    for copy in weights:
        start(copy)

    def near(_):
        ring_wait(own_ring, 1)
        ring_wait(own_ring, 7)
        spread(-1)
        spread(1)
        x_copy(3, 0).wait_recv()
        ring_first(far_ring)
        ring_second(own_ring)
        spread(2)
        spread(-2)

    def rest(_):
        for number in (3, 5, 4):
            ring_wait(own_ring, number)
            spread(-number)

    def fetch(chunk):
        column, part = chunk // 2, chunk % 2
        for origin in SLOTS[part * blocks : (part + 1) * blocks]:
            if column in (1, 2):
                x_copy(BACK[column], slot(origin)).wait_recv()
            elif column == 3 and origin in (1, -1, 3, -3, 4):
                ring_wait(far_ring, -origin % 8)
        start(twin_copy(chunk))

    def pair_copy(chunk, side):
        return remote(
            sb.at[chunk, pl.ds(2 * side, 2)], (pa, pb)[side].at[chunk],
            b_send.at[chunk, side], b_recv.at[chunk, side], y_peer((1, -1)[side]),
        )

    def far_copy(chunk):
        return remote(sb.at[chunk, 4], pc.at[chunk], b_send.at[chunk, 2], b_recv.at[chunk, 2], y_peer(-far))

    def join_copy(chunk, side):
        return remote(
            sc.at[chunk, side], rc.at[chunk, side],
            b_send.at[chunk, 3 + side], b_recv.at[chunk, 3 + side], y_peer((2, -2)[side]),
        )

    def add_features(chunk):
        column, slots = chunk // 2, pl.ds(chunk % 2 * blocks, blocks)
        ours = xg[k, column, slots]
        left = ours[:, 0].reshape(rows, width)
        left_grad = ours[:, 1].reshape(rows, width)
        xo[0, chunk] = left
        xo[1, chunk] = left_grad
        sums = [
            dot(left, wgv[k], 1, 0),
            dot(left, wuv[k], 1, 0),
            dot(left_grad, wdv[k], 1, 1),
        ]
        if chunk == 0:
            for copy in weights:
                copy.wait_recv()
        twin_copy(chunk).wait_recv()
        other = xg[1 - k, column, slots]
        right = other[:, 0].reshape(rows, width)
        right_grad = other[:, 1].reshape(rows, width)
        sums[0] += dot(right, wgs[...], 1, 0)
        sums[1] += dot(right, wus[...], 1, 0)
        sums[2] += dot(right_grad, wds[...], 1, 1)
        for part in range(3):
            cols = pl.ds(part * cut, cut)
            for side in range(2):
                pf[chunk, :, pl.ds(side * share, share), cols] = sums[part][:, side * cut : (side + 1) * cut].reshape(
                    ny, share, cut
                )
        for index, step in enumerate((1, 3, -1, -3, 4)):
            sb[chunk, index] = encode(pf[chunk, along_y(step)], SUM_SCALE)
        start(far_copy(chunk))
        start(pair_copy(chunk, 0))
        start(pair_copy(chunk, 1))

    def join(chunk):
        pair_copy(chunk, 0).wait_recv()
        pair_copy(chunk, 1).wait_recv()
        far_copy(chunk).wait_recv()
        distant = decode(pc[chunk], SUM_SCALE)
        second = k.astype(jnp.float32)
        ahead = pf[chunk, along_y(2)] + decode(pa[chunk, 1], SUM_SCALE) + distant * second
        behind = pf[chunk, along_y(-2)] + decode(pb[chunk, 1], SUM_SCALE) + distant * (1.0 - second)
        sc[chunk, 0] = encode(ahead, SUM_SCALE)
        sc[chunk, 1] = encode(behind, SUM_SCALE)
        start(join_copy(chunk, 0))
        start(join_copy(chunk, 1))

    def y_ring(chunk):
        def mine(origin):
            return along_y(-far if origin is None else origin)

        return (hb.at[chunk, k], mine, lambda origin, _: mine(origin), y_peer, c_send.at[chunk], c_recv.at[chunk])

    def half_copy(chunk):
        ours = hb.at[chunk, k]
        return remote(ours, ours, cs_send.at[chunk], cs_recv.at[chunk], sibling)

    def gate(chunk):
        join_copy(chunk, 0).wait_recv()
        join_copy(chunk, 1).wait_recv()
        total = pf[chunk, y] + decode(pa[chunk, 0], SUM_SCALE) + decode(pb[chunk, 0], SUM_SCALE)
        total += decode(rc[chunk, 0], SUM_SCALE) + decode(rc[chunk, 1], SUM_SCALE)
        gate_pre = total[:, :cut]
        up_pre = total[:, cut : 2 * cut]
        hidden_delta = total[:, 2 * cut :]
        sigma = jax.nn.sigmoid(gate_pre)
        silu_gate = gate_pre * sigma
        slope = sigma * (1.0 + gate_pre * (1.0 - sigma))
        hb[chunk, k, y, 0] = (silu_gate * up_pre).astype(jnp.bfloat16)
        hb[chunk, k, y, 1] = (hidden_delta * up_pre * slope).astype(jnp.bfloat16)
        hb[chunk, k, y, 2] = (hidden_delta * silu_gate).astype(jnp.bfloat16)
        ring_first(y_ring(chunk))

    def block_copy(column, chunk, index):
        step = SLOTS[index] % nz
        return remote(
            ib.at[chunk, index % blocks], jb.at[BACK[column], step],
            dx_send.at[column, step], dx_recv.at[BACK[column], step], plane_peer(step, OFFSETS[column]),
        )

    def term(chunk, side):
        for array in range(3):
            pieces = hb[chunk, side, :, array].astype(jnp.float32)
            first = pieces[:, :share].reshape(rows, cut)
            second = pieces[:, share:].reshape(rows, cut)
            ho[array, side, chunk] = jnp.concatenate([first, second], axis=1).astype(jnp.bfloat16)
        return dot(ho[1, side, chunk], wgv[side], 1, 1) + dot(ho[2, side, chunk], wuv[side], 1, 1)

    def share_half(chunk):
        for number in (1, 7, 3, 5, 4):
            ring_wait(y_ring(chunk), number)
        start(half_copy(chunk))

    def grad(chunk):
        total = term(chunk, k)
        half_copy(chunk).wait_recv()
        total = (total + term(chunk, 1 - k)).reshape(blocks, block, width)
        if chunk == 1:
            tail[...] = total
            return
        ib[chunk] = encode(total, GRAD_SCALE)
        if chunk == 0:
            own[...] = total[0]
        if chunk in (3, 5):
            start(column_copy(chunk // 2))
        else:
            send_blocks(chunk)

    def send_blocks(chunk):
        column, part = chunk // 2, chunk % 2
        for index in reversed(range(part * blocks, (part + 1) * blocks)):
            if column or index:
                start(block_copy(column, chunk, index))

    def column_copy(column):
        return remote(
            ib.at[2 * column + 1], mb.at[BACK[column] - 1],
            mx_send.at[column - 1], mx_recv.at[BACK[column] - 1], x_peer(OFFSETS[column]),
        )

    def merge(chunk):
        total = tail[...]
        for column in (1, 2):
            column_copy(BACK[column]).wait_recv()
            total += decode(mb[column - 1], GRAD_SCALE)
        ib[chunk] = encode(total, GRAD_SCALE)
        send_blocks(chunk)

    actions = {
        "near": near, "far": lambda _: ring_second(far_ring), "rest": rest,
        "fetch": fetch, "sum": add_features, "join": join, "gate": gate,
        "pass": lambda chunk: ring_second(y_ring(chunk)), "half": share_half, "grad": grad,
        "merge": merge,
    }
    for step in STEPS:
        actions[step[:-1]](int(step[-1]))

    tokens = 2 * nx * rows
    left = xo[0].reshape(tokens, width)
    for side in range(2):
        cols = pl.ds(side * half, half)
        ggv[:, cols] = dot(left, ho[1, side].reshape(tokens, half), 0, 0).astype(jnp.bfloat16)
        ugv[:, cols] = dot(left, ho[2, side].reshape(tokens, half), 0, 0).astype(jnp.bfloat16)
    stores = [
        pltpu.make_async_copy(ggv, gg_out, load_sem.at[0]),
        pltpu.make_async_copy(ugv, ug_out, load_sem.at[1]),
        pltpu.make_async_copy(dgv, dg_out, load_sem.at[2]),
        pltpu.make_async_copy(igv, ig_out, load_sem.at[3]),
    ]
    stores[0].start()
    stores[1].start()
    right = xo[1].reshape(tokens, width)
    for side in range(2):
        cols = pl.ds(side * half, half)
        dgv[cols] = dot(ho[0, side].reshape(tokens, half), right, 0, 0).astype(jnp.bfloat16)
    stores[2].start()

    for copy in sent:
        copy.wait_send()
    total = own[...]
    for column in (1, 2, 3, 0):
        for index in range(nz if column in (0, 3) else blocks):
            if column or index:
                block_copy(BACK[column], 0, index).wait_recv()
                total += decode(jb[column, SLOTS[index] % nz], GRAD_SCALE)
    igv[...] = total.astype(jnp.bfloat16)
    stores[3].start()
    for store in stores:
        store.wait()


def hand_over(*refs):
    count = len(refs) // 3
    given, out, held, sems = refs[:count], refs[count : 2 * count], refs[2 * count : 3 * count], refs[-1]
    loads = [pltpu.make_async_copy(given[i], held[i], sems.at[0, i]) for i in range(count)]
    stores = [pltpu.make_async_copy(held[i], out[i], sems.at[1, i]) for i in range(count)]
    for load in loads:
        load.start()
    for load, store in zip(loads, stores):
        load.wait()
        store.start()
    for store in stores:
        store.wait()


def shards(ny, nz, tokens, grad_output, gate_weight, up_weight, down_weight):
    block, width = tokens.shape
    hidden = gate_weight.shape[1] // 2
    half = hidden // 2
    nx = 4
    chunks, rows, cut = 2 * nx, nz // 2 * block, half // 2
    bf16, f32 = jnp.bfloat16, jnp.float32
    vmem, dma = pltpu.VMEM, pltpu.SemaphoreType.DMA
    results = (
        jax.ShapeDtypeStruct((block, width), bf16),
        jax.ShapeDtypeStruct((width, hidden), bf16),
        jax.ShapeDtypeStruct((width, hidden), bf16),
        jax.ShapeDtypeStruct((hidden, width), bf16),
    )
    made = pl.pallas_call(
        functools.partial(kernel, ny, nz),
        out_shape=results,
        in_specs=[pl.BlockSpec(memory_space=pl.ANY)] * 5,
        out_specs=[pl.BlockSpec(memory_space=pl.ANY)] * 4,
        scratch_shapes=[
            vmem((2, nx, nz, 2, block, width), bf16),
            vmem((2, width, half), bf16),
            vmem((2, width, half), bf16),
            vmem((2, half, width), bf16),
            vmem((width, half), bf16),
            vmem((width, half), bf16),
            vmem((half, width), bf16),
            vmem((2, chunks, rows, width), bf16),
            vmem((chunks, ny, block, 3 * cut), f32),
            vmem((chunks, 5, block, 3 * cut), bf16),
            vmem((chunks, 2, block, 3 * cut), bf16),
            vmem((chunks, 2, block, 3 * cut), bf16),
            vmem((chunks, block, 3 * cut), bf16),
            vmem((chunks, 2, block, 3 * cut), bf16),
            vmem((chunks, 2, block, 3 * cut), bf16),
            vmem((chunks, 2, ny, 3, block, cut), bf16),
            vmem((3, 2, chunks, rows, half), bf16),
            vmem((block, width), f32),
            vmem((chunks, nz // 2, block, width), bf16),
            vmem((nx, nz, block, width), bf16),
            vmem((2, nz // 2, block, width), bf16),
            vmem((nz // 2, block, width), f32),
            vmem((width, hidden), bf16),
            vmem((width, hidden), bf16),
            vmem((hidden, width), bf16),
            vmem((block, width), bf16),
            dma((8,)),
            dma((2, nz)), dma((2, nz)),
            dma((nx, nz)), dma((nx, nz)),
            dma((chunks,)), dma((chunks,)),
            dma((3,)), dma((3,)),
            dma((chunks, 5)), dma((chunks, 5)),
            dma((chunks, ny)), dma((chunks, ny)),
            dma((chunks,)), dma((chunks,)),
            dma((nx, nz)), dma((nx, nz)),
            dma((2,)), dma((2,)),
        ],
        compiler_params=pltpu.CompilerParams(
            collective_id=0, has_side_effects=True, vmem_limit_bytes=60 * 2**20
        ),
        name="ffn_backward",
    )(tokens, grad_output, gate_weight, up_weight, down_weight)
    return pl.pallas_call(
        hand_over,
        out_shape=results,
        in_specs=[pl.BlockSpec(memory_space=pl.ANY)] * 4,
        out_specs=[pl.BlockSpec(memory_space=pl.ANY)] * 4,
        scratch_shapes=[vmem(result.shape, bf16) for result in results] + [dma((2, 4))],
        compiler_params=pltpu.CompilerParams(vmem_limit_bytes=60 * 2**20),
        name="hand_over",
    )(*made)


def solution(mesh):
    placed = (
        P(("col", "depth"), "row"),
        P(("col", "depth"), "row"),
        P("row", "col"),
        P("row", "col"),
        P("col", "row"),
    )
    ny, nz = mesh.shape["row"] // 2, mesh.shape["col"] // 2
    return jax.shard_map(
        functools.partial(shards, ny, nz),
        mesh=mesh,
        in_specs=placed,
        out_specs=(
            P(("col", "depth"), "row"),
            P("row", ("col", "depth")),
            P("row", ("col", "depth")),
            P(("col", "depth"), "row"),
        ),
        check_vma=False,
    )
```

```python
import functools

import jax
import jax.numpy as jnp
from jax import lax
from jax.experimental import pallas as pl
from jax.experimental.pallas import tpu as pltpu
from jax.sharding import PartitionSpec as P

MESH = pl.DeviceIdType.MESH
OFFSETS = (0, 1, 3, 2)
BACK = (0, 2, 1, 3)
SLOTS = (0, 1, -1, 2, -2, 3, -3, 4)
SUM_SCALE = 2.0**48
GRAD_SCALE = 2.0**30


def encode(value, scale):
    scaled = value * scale
    return (scaled * jnp.abs(scaled)).astype(jnp.bfloat16)


def decode(code, scale):
    wide = code.astype(jnp.float32)
    root = jnp.sqrt(jnp.abs(wide)) * (1.0 / scale)
    return jnp.where(wide < 0.0, -root, root)


def dot(left, right, left_dim, right_dim):
    return lax.dot_general(
        left, right, (((left_dim,), (right_dim,)), ((), ())), preferred_element_type=jnp.float32
    )


STEPS = (
    "near0", "fetch0", "sum0", "fetch2", "fetch4", "far0", "rest0", "sum2", "sum4", "fetch6", "fetch1", "join0",
    "sum6", "sum1", "join2", "join4", "fetch3", "fetch5", "fetch7", "gate0", "join6", "sum3", "sum5", "sum7",
    "join1", "gate2", "gate4", "pass0", "join3", "join5", "join7", "gate6", "pass2", "pass4", "gate3", "half0",
    "pass6", "gate5", "gate7", "gate1", "grad0", "half2", "half4", "grad2", "pass3", "grad4", "half6", "pass5",
    "pass7", "pass1", "grad6", "half3", "half5", "grad3", "half7", "grad5", "half1", "grad7", "grad1", "merge1",
)


def kernel(
    ny, nz,
    tok, grd, wg, wu, wd,
    ig_out, gg_out, ug_out, dg_out,
    xg, wgv, wuv, wdv, wgs, wus, wds, wgt, wut, wdt, xo, pf, sb, pa, pb, pc, sc, rc, hb, ho, own, ib, jb, mb, tail, ggv, ugv, dgv, igv,
    load_sem, az_send, az_recv, ax_send, ax_recv, as_send, as_recv, ws_send, ws_recv,
    b_send, b_recv, c_send, c_recv, cs_send, cs_recv, dx_send, dx_recv, mx_send, mx_recv,
):
    nx = 4
    block, width = tok.shape
    half = wgv.shape[2]
    blocks = nz // 2
    rows = blocks * block
    share = rows // ny
    cut = half // 2
    r, q, d = lax.axis_index("row"), lax.axis_index("col"), lax.axis_index("depth")
    y, k = r // 2, lax.rem(r, 2)
    z, x = q // 2, d * 2 + lax.rem(q, 2)

    def place(py, pz, px, pk):
        return (py * 2 + pk, pz * 2 + lax.rem(px, 2), px // 2)

    def along_y(step):
        return lax.rem(y + step + ny, ny)

    def along_z(step):
        return lax.rem(z + step + nz, nz)

    def y_peer(step):
        return place(along_y(step), z, x, k)

    def plane_peer(step, across):
        return place(y, along_z(step), lax.rem(x + across, nx), k)

    def z_peer(step):
        return plane_peer(step, 0)

    def x_peer(across):
        return plane_peer(0, across)

    sibling = place(y, z, x, 1 - k)
    far = 2 - 4 * k
    sent = []

    def remote(src, dst, send, recv, device):
        return pltpu.make_async_remote_copy(
            src_ref=src, dst_ref=dst, send_sem=send, recv_sem=recv, device_id=device, device_id_type=MESH
        )

    def start(copy):
        copy.start()
        sent.append(copy)

    loads = [
        pltpu.make_async_copy(tok, xg.at[k, 0, 0, 0], load_sem.at[0]),
        pltpu.make_async_copy(grd, xg.at[k, 0, 0, 1], load_sem.at[1]),
    ]
    for side in range(2):
        first = pl.multiple_of(d * (2 * half) + side * half, half)
        loads += [
            pltpu.make_async_copy(wg.at[:, pl.ds(first, half)], wgv.at[side], load_sem.at[2 + side]),
            pltpu.make_async_copy(wu.at[:, pl.ds(first, half)], wuv.at[side], load_sem.at[4 + side]),
            pltpu.make_async_copy(wd.at[pl.ds(first, half)], wdv.at[side], load_sem.at[6 + side]),
        ]
    for load in loads:
        load.start()

    barrier = pltpu.get_barrier_semaphore()
    friends = [sibling]
    friends += [z_peer(step) for step in (1, -1, 2, -2)]
    friends += [x_peer(across) for across in range(1, nx)]
    friends += [y_peer(step) for step in (1, -1, 2, -2)]
    for device in friends:
        pl.semaphore_signal(barrier, inc=1, device_id=device, device_id_type=MESH)
    loads[0].wait()
    loads[1].wait()
    pl.semaphore_wait(barrier, len(friends))

    def ring_copy(ring, origin, number, target):
        buffer, mine, theirs, peer, send, recv = ring
        return remote(
            buffer.at[mine(origin)], buffer.at[theirs(origin, number)], send.at[number], recv.at[number], peer(target)
        )

    def ring_first(ring):
        for target in (2, -2, 1, -1):
            start(ring_copy(ring, 0, target % 8, target))

    def ring_second(ring):
        ring_wait(ring, 2)
        ring_wait(ring, 6)
        start(ring_copy(ring, None, 4, far))
        start(ring_copy(ring, -2, 3, 1))
        start(ring_copy(ring, 2, 5, -1))

    def ring_wait(ring, number):
        buffer, mine, theirs, peer, send, recv = ring
        place_of = buffer.at[theirs(-number, number)]
        remote(place_of, place_of, send.at[number], recv.at[number], peer(1)).wait_recv()

    def slot(origin):
        return SLOTS.index((origin + 3) % 8 - 3)

    def z_mine(origin):
        return slot(2) * k + slot(-2) * (1 - k) if origin is None else slot(origin)

    def z_ring(column, which):
        return (
            xg.at[k, column], z_mine, lambda origin, number: slot(-number), z_peer, az_send.at[which], az_recv.at[which]
        )

    own_ring, far_ring = z_ring(0, 0), z_ring(3, 1)

    def x_copy(column, at):
        return remote(
            xg.at[k, 0, at], xg.at[k, BACK[column], at],
            ax_send.at[column, at], ax_recv.at[BACK[column], at], x_peer(OFFSETS[column]),
        )

    def twin_copy(chunk):
        ours = xg.at[k, chunk // 2, pl.ds(chunk % 2 * blocks, blocks)]
        return remote(ours, ours, as_send.at[chunk], as_recv.at[chunk], sibling)

    def spread(origin):
        for column in (1, 2):
            start(x_copy(column, slot(origin)))

    start(x_copy(3, 0))
    ring_first(own_ring)
    spread(0)
    for load in loads[2:]:
        load.wait()
    weights = [
        remote(wgv.at[1 - k], wgs, ws_send.at[0], ws_recv.at[0], sibling),
        remote(wuv.at[1 - k], wus, ws_send.at[1], ws_recv.at[1], sibling),
        remote(wdt.at[1 - k], wds, ws_send.at[2], ws_recv.at[2], sibling),
    ]
    start(weights[0])
    start(weights[1])
    wdt[1 - k] = wdv[1 - k].T
    start(weights[2])
    wdt[k] = wdv[k].T
    for side in range(2):
        wgt[side] = wgv[side].T
        wut[side] = wuv[side].T

    def near(_):
        ring_wait(own_ring, 1)
        ring_wait(own_ring, 7)
        spread(-1)
        spread(1)
        x_copy(3, 0).wait_recv()
        ring_first(far_ring)
        ring_second(own_ring)
        spread(2)
        spread(-2)

    def rest(_):
        for number in (3, 5, 4):
            ring_wait(own_ring, number)
            spread(-number)

    def fetch(chunk):
        column, part = chunk // 2, chunk % 2
        for origin in SLOTS[part * blocks : (part + 1) * blocks]:
            if column in (1, 2):
                x_copy(BACK[column], slot(origin)).wait_recv()
            elif column == 3 and origin in (1, -1, 3, -3, 4):
                ring_wait(far_ring, -origin % 8)
        start(twin_copy(chunk))

    def pair_copy(chunk, side):
        return remote(
            sb.at[chunk, pl.ds(2 * side, 2)], (pa, pb)[side].at[chunk],
            b_send.at[chunk, side], b_recv.at[chunk, side], y_peer((1, -1)[side]),
        )

    def far_copy(chunk):
        return remote(sb.at[chunk, 4], pc.at[chunk], b_send.at[chunk, 2], b_recv.at[chunk, 2], y_peer(-far))

    def join_copy(chunk, side):
        return remote(
            sc.at[chunk, side], rc.at[chunk, side],
            b_send.at[chunk, 3 + side], b_recv.at[chunk, 3 + side], y_peer((2, -2)[side]),
        )

    def add_features(chunk):
        column, slots = chunk // 2, pl.ds(chunk % 2 * blocks, blocks)
        ours = xg[k, column, slots]
        left = ours[:, 0].reshape(rows, width)
        left_grad = ours[:, 1].reshape(rows, width)
        xo[0, chunk] = left
        xo[1, chunk] = left_grad
        sums = [
            dot(left, wgv[k], 1, 0),
            dot(left, wuv[k], 1, 0),
            dot(left_grad, wdt[k], 1, 0),
        ]
        if chunk == 0:
            for copy in weights:
                copy.wait_recv()
        twin_copy(chunk).wait_recv()
        other = xg[1 - k, column, slots]
        right = other[:, 0].reshape(rows, width)
        right_grad = other[:, 1].reshape(rows, width)
        sums[0] += dot(right, wgs[...], 1, 0)
        sums[1] += dot(right, wus[...], 1, 0)
        sums[2] += dot(right_grad, wds[...], 1, 0)
        for part in range(3):
            cols = pl.ds(part * cut, cut)
            for side in range(2):
                pf[chunk, :, pl.ds(side * share, share), cols] = sums[part][:, side * cut : (side + 1) * cut].reshape(
                    ny, share, cut
                )
        for index, step in enumerate((1, 3, -1, -3, 4)):
            sb[chunk, index] = encode(pf[chunk, along_y(step)], SUM_SCALE)
        start(far_copy(chunk))
        start(pair_copy(chunk, 0))
        start(pair_copy(chunk, 1))

    def join(chunk):
        pair_copy(chunk, 0).wait_recv()
        pair_copy(chunk, 1).wait_recv()
        far_copy(chunk).wait_recv()
        distant = decode(pc[chunk], SUM_SCALE)
        second = k.astype(jnp.float32)
        ahead = pf[chunk, along_y(2)] + decode(pa[chunk, 1], SUM_SCALE) + distant * second
        behind = pf[chunk, along_y(-2)] + decode(pb[chunk, 1], SUM_SCALE) + distant * (1.0 - second)
        sc[chunk, 0] = encode(ahead, SUM_SCALE)
        sc[chunk, 1] = encode(behind, SUM_SCALE)
        start(join_copy(chunk, 0))
        start(join_copy(chunk, 1))

    def y_ring(chunk):
        def mine(origin):
            return along_y(-far if origin is None else origin)

        return (hb.at[chunk, k], mine, lambda origin, _: mine(origin), y_peer, c_send.at[chunk], c_recv.at[chunk])

    def half_copy(chunk):
        ours = hb.at[chunk, k]
        return remote(ours, ours, cs_send.at[chunk], cs_recv.at[chunk], sibling)

    def gate(chunk):
        join_copy(chunk, 0).wait_recv()
        join_copy(chunk, 1).wait_recv()
        total = pf[chunk, y] + decode(pa[chunk, 0], SUM_SCALE) + decode(pb[chunk, 0], SUM_SCALE)
        total += decode(rc[chunk, 0], SUM_SCALE) + decode(rc[chunk, 1], SUM_SCALE)
        gate_pre = total[:, :cut]
        up_pre = total[:, cut : 2 * cut]
        hidden_delta = total[:, 2 * cut :]
        sigma = jax.nn.sigmoid(gate_pre)
        silu_gate = gate_pre * sigma
        slope = sigma * (1.0 + gate_pre * (1.0 - sigma))
        hb[chunk, k, y, 0] = (silu_gate * up_pre).astype(jnp.bfloat16)
        hb[chunk, k, y, 1] = (hidden_delta * up_pre * slope).astype(jnp.bfloat16)
        hb[chunk, k, y, 2] = (hidden_delta * silu_gate).astype(jnp.bfloat16)
        ring_first(y_ring(chunk))

    def block_copy(column, chunk, index):
        step = SLOTS[index] % nz
        return remote(
            ib.at[chunk, index % blocks], jb.at[BACK[column], step],
            dx_send.at[column, step], dx_recv.at[BACK[column], step], plane_peer(step, OFFSETS[column]),
        )

    def term(chunk, side):
        for array in range(3):
            pieces = hb[chunk, side, :, array].astype(jnp.float32)
            first = pieces[:, :share].reshape(rows, cut)
            second = pieces[:, share:].reshape(rows, cut)
            ho[array, side, chunk] = jnp.concatenate([first, second], axis=1).astype(jnp.bfloat16)
        return dot(ho[1, side, chunk], wgt[side], 1, 0) + dot(ho[2, side, chunk], wut[side], 1, 0)

    def share_half(chunk):
        for number in (1, 7, 3, 5, 4):
            ring_wait(y_ring(chunk), number)
        start(half_copy(chunk))

    def grad(chunk):
        total = term(chunk, k)
        half_copy(chunk).wait_recv()
        total = (total + term(chunk, 1 - k)).reshape(blocks, block, width)
        if chunk == 1:
            tail[...] = total
            return
        ib[chunk] = encode(total, GRAD_SCALE)
        if chunk == 0:
            own[...] = total[0]
        if chunk in (3, 5):
            start(column_copy(chunk // 2))
        else:
            send_blocks(chunk)

    def send_blocks(chunk):
        column, part = chunk // 2, chunk % 2
        for index in reversed(range(part * blocks, (part + 1) * blocks)):
            if column or index:
                start(block_copy(column, chunk, index))

    def column_copy(column):
        return remote(
            ib.at[2 * column + 1], mb.at[BACK[column] - 1],
            mx_send.at[column - 1], mx_recv.at[BACK[column] - 1], x_peer(OFFSETS[column]),
        )

    def merge(chunk):
        total = tail[...]
        for column in (1, 2):
            column_copy(BACK[column]).wait_recv()
            total += decode(mb[column - 1], GRAD_SCALE)
        ib[chunk] = encode(total, GRAD_SCALE)
        send_blocks(chunk)

    actions = {
        "near": near, "far": lambda _: ring_second(far_ring), "rest": rest,
        "fetch": fetch, "sum": add_features, "join": join, "gate": gate,
        "pass": lambda chunk: ring_second(y_ring(chunk)), "half": share_half, "grad": grad,
        "merge": merge,
    }
    for step in STEPS:
        actions[step[:-1]](int(step[-1]))

    tokens = 2 * nx * rows
    left = xo[0].reshape(tokens, width)
    for side in range(2):
        cols = pl.ds(side * half, half)
        ggv[:, cols] = dot(left, ho[1, side].reshape(tokens, half), 0, 0).astype(jnp.bfloat16)
        ugv[:, cols] = dot(left, ho[2, side].reshape(tokens, half), 0, 0).astype(jnp.bfloat16)
    stores = [
        pltpu.make_async_copy(ggv, gg_out, load_sem.at[0]),
        pltpu.make_async_copy(ugv, ug_out, load_sem.at[1]),
        pltpu.make_async_copy(dgv, dg_out, load_sem.at[2]),
        pltpu.make_async_copy(igv, ig_out, load_sem.at[3]),
    ]
    stores[0].start()
    stores[1].start()
    right = xo[1].reshape(tokens, width)
    for side in range(2):
        cols = pl.ds(side * half, half)
        dgv[cols] = dot(ho[0, side].reshape(tokens, half), right, 0, 0).astype(jnp.bfloat16)
    stores[2].start()

    for copy in sent:
        copy.wait_send()
    total = own[...]
    for column in (1, 2, 3, 0):
        for index in range(nz if column in (0, 3) else blocks):
            if column or index:
                block_copy(BACK[column], 0, index).wait_recv()
                total += decode(jb[column, SLOTS[index] % nz], GRAD_SCALE)
    igv[...] = total.astype(jnp.bfloat16)
    stores[3].start()
    for store in stores:
        store.wait()


def hand_over(*refs):
    count = len(refs) // 3
    given, out, held, sems = refs[:count], refs[count : 2 * count], refs[2 * count : 3 * count], refs[-1]
    loads = [pltpu.make_async_copy(given[i], held[i], sems.at[0, i]) for i in range(count)]
    stores = [pltpu.make_async_copy(held[i], out[i], sems.at[1, i]) for i in range(count)]
    for load in loads:
        load.start()
    for load, store in zip(loads, stores):
        load.wait()
        store.start()
    for store in stores:
        store.wait()


def shards(ny, nz, tokens, grad_output, gate_weight, up_weight, down_weight):
    block, width = tokens.shape
    hidden = gate_weight.shape[1] // 2
    half = hidden // 2
    nx = 4
    chunks, rows, cut = 2 * nx, nz // 2 * block, half // 2
    bf16, f32 = jnp.bfloat16, jnp.float32
    vmem, dma = pltpu.VMEM, pltpu.SemaphoreType.DMA
    results = (
        jax.ShapeDtypeStruct((block, width), bf16),
        jax.ShapeDtypeStruct((width, hidden), bf16),
        jax.ShapeDtypeStruct((width, hidden), bf16),
        jax.ShapeDtypeStruct((hidden, width), bf16),
    )
    made = pl.pallas_call(
        functools.partial(kernel, ny, nz),
        out_shape=results,
        in_specs=[pl.BlockSpec(memory_space=pl.ANY)] * 5,
        out_specs=[pl.BlockSpec(memory_space=pl.ANY)] * 4,
        scratch_shapes=[
            vmem((2, nx, nz, 2, block, width), bf16),
            vmem((2, width, half), bf16),
            vmem((2, width, half), bf16),
            vmem((2, half, width), bf16),
            vmem((width, half), bf16),
            vmem((width, half), bf16),
            vmem((width, half), bf16),
            vmem((2, half, width), bf16),
            vmem((2, half, width), bf16),
            vmem((2, width, half), bf16),
            vmem((2, chunks, rows, width), bf16),
            vmem((chunks, ny, block, 3 * cut), f32),
            vmem((chunks, 5, block, 3 * cut), bf16),
            vmem((chunks, 2, block, 3 * cut), bf16),
            vmem((chunks, 2, block, 3 * cut), bf16),
            vmem((chunks, block, 3 * cut), bf16),
            vmem((chunks, 2, block, 3 * cut), bf16),
            vmem((chunks, 2, block, 3 * cut), bf16),
            vmem((chunks, 2, ny, 3, block, cut), bf16),
            vmem((3, 2, chunks, rows, half), bf16),
            vmem((block, width), f32),
            vmem((chunks, nz // 2, block, width), bf16),
            vmem((nx, nz, block, width), bf16),
            vmem((2, nz // 2, block, width), bf16),
            vmem((nz // 2, block, width), f32),
            vmem((width, hidden), bf16),
            vmem((width, hidden), bf16),
            vmem((hidden, width), bf16),
            vmem((block, width), bf16),
            dma((8,)),
            dma((2, nz)), dma((2, nz)),
            dma((nx, nz)), dma((nx, nz)),
            dma((chunks,)), dma((chunks,)),
            dma((3,)), dma((3,)),
            dma((chunks, 5)), dma((chunks, 5)),
            dma((chunks, ny)), dma((chunks, ny)),
            dma((chunks,)), dma((chunks,)),
            dma((nx, nz)), dma((nx, nz)),
            dma((2,)), dma((2,)),
        ],
        compiler_params=pltpu.CompilerParams(
            collective_id=0, has_side_effects=True, vmem_limit_bytes=60 * 2**20
        ),
        name="ffn_backward",
    )(tokens, grad_output, gate_weight, up_weight, down_weight)
    return pl.pallas_call(
        hand_over,
        out_shape=results,
        in_specs=[pl.BlockSpec(memory_space=pl.ANY)] * 4,
        out_specs=[pl.BlockSpec(memory_space=pl.ANY)] * 4,
        scratch_shapes=[vmem(result.shape, bf16) for result in results] + [dma((2, 4))],
        compiler_params=pltpu.CompilerParams(vmem_limit_bytes=60 * 2**20),
        name="hand_over",
    )(*made)


def solution(mesh):
    placed = (
        P(("col", "depth"), "row"),
        P(("col", "depth"), "row"),
        P("row", "col"),
        P("row", "col"),
        P("col", "row"),
    )
    ny, nz = mesh.shape["row"] // 2, mesh.shape["col"] // 2
    return jax.shard_map(
        functools.partial(shards, ny, nz),
        mesh=mesh,
        in_specs=placed,
        out_specs=(
            P(("col", "depth"), "row"),
            P("row", ("col", "depth")),
            P("row", ("col", "depth")),
            P(("col", "depth"), "row"),
        ),
        check_vma=False,
    )
```

```python
import functools

import jax
import jax.numpy as jnp
from jax import lax
from jax.experimental import pallas as pl
from jax.experimental.pallas import tpu as pltpu
from jax.sharding import PartitionSpec as P

MESH = pl.DeviceIdType.MESH
OFFSETS = (0, 1, 3, 2)
BACK = (0, 2, 1, 3)
SLOTS = (0, 1, -1, 2, -2, 3, -3, 4)
SUM_SCALE = 2.0**48
GRAD_SCALE = 2.0**30


def encode(value, scale):
    scaled = value * scale
    return (scaled * jnp.abs(scaled)).astype(jnp.bfloat16)


def decode(code, scale):
    wide = code.astype(jnp.float32)
    root = jnp.sqrt(jnp.abs(wide)) * (1.0 / scale)
    return jnp.where(wide < 0.0, -root, root)


def dot(left, right, left_dim, right_dim):
    return lax.dot_general(
        left, right, (((left_dim,), (right_dim,)), ((), ())), preferred_element_type=jnp.float32
    )


LAST = 1
STEPS = (
    "near0", "fetch0", "sum0", "fetch2", "fetch4", "far0", "rest0", "sum2", "sum4", "fetch6", "fetch1", "join0",
    "sum6", "sum1", "join2", "join4", "fetch3", "fetch5", "fetch7", "gate0", "join6", "sum3", "sum5", "sum7",
    "join1", "gate2", "gate4", "pass0", "join3", "join5", "join7", "gate6", "pass2", "pass4", "gate3", "half0",
    "pass6", "gate5", "gate7", "gate1", "grad0", "half2", "half4", "grad2", "pass3", "grad4", "half6", "pass5",
    "pass7", "grad6", "half3", "half5", "grad3", "half7", "grad5", "half1", "grad7", "grad1", "merge1",
)


def kernel(
    ny, nz,
    tok, grd, wg, wu, wd,
    ig_out, gg_out, ug_out, dg_out,
    xg, wgv, wuv, wdv, wgs, wus, wds, wgt, wut, wdt, xo, pf, sb, pa, pb, pc, sc, rc, hb, ho, own, ib, jb, mb, tail, ggv, ugv, dgv, igv,
    load_sem, az_send, az_recv, ax_send, ax_recv, as_send, as_recv, ws_send, ws_recv,
    b_send, b_recv, c_send, c_recv, cs_send, cs_recv, dx_send, dx_recv, mx_send, mx_recv,
):
    nx = 4
    block, width = tok.shape
    half = wgv.shape[2]
    blocks = nz // 2
    rows = blocks * block
    share = rows // ny
    cut = half // 2
    r, q, d = lax.axis_index("row"), lax.axis_index("col"), lax.axis_index("depth")
    y, k = r // 2, lax.rem(r, 2)
    z, x = q // 2, d * 2 + lax.rem(q, 2)

    def place(py, pz, px, pk):
        return (py * 2 + pk, pz * 2 + lax.rem(px, 2), px // 2)

    def along_y(step):
        return lax.rem(y + step + ny, ny)

    def along_z(step):
        return lax.rem(z + step + nz, nz)

    def y_peer(step):
        return place(along_y(step), z, x, k)

    def plane_peer(step, across):
        return place(y, along_z(step), lax.rem(x + across, nx), k)

    def z_peer(step):
        return plane_peer(step, 0)

    def x_peer(across):
        return plane_peer(0, across)

    sibling = place(y, z, x, 1 - k)
    far = 2 - 4 * k
    sent = []

    def remote(src, dst, send, recv, device):
        return pltpu.make_async_remote_copy(
            src_ref=src, dst_ref=dst, send_sem=send, recv_sem=recv, device_id=device, device_id_type=MESH
        )

    def start(copy):
        copy.start()
        sent.append(copy)

    loads = [
        pltpu.make_async_copy(tok, xg.at[k, 0, 0, 0], load_sem.at[0]),
        pltpu.make_async_copy(grd, xg.at[k, 0, 0, 1], load_sem.at[1]),
    ]
    for side in range(2):
        first = pl.multiple_of(d * (2 * half) + side * half, half)
        loads += [
            pltpu.make_async_copy(wg.at[:, pl.ds(first, half)], wgv.at[side], load_sem.at[2 + side]),
            pltpu.make_async_copy(wu.at[:, pl.ds(first, half)], wuv.at[side], load_sem.at[4 + side]),
            pltpu.make_async_copy(wd.at[pl.ds(first, half)], wdv.at[side], load_sem.at[6 + side]),
        ]
    for load in loads:
        load.start()

    barrier = pltpu.get_barrier_semaphore()
    friends = [sibling]
    friends += [z_peer(step) for step in (1, -1, 2, -2)]
    friends += [x_peer(across) for across in range(1, nx)]
    friends += [y_peer(step) for step in (1, -1, 2, -2)]
    for device in friends:
        pl.semaphore_signal(barrier, inc=1, device_id=device, device_id_type=MESH)
    loads[0].wait()
    loads[1].wait()
    pl.semaphore_wait(barrier, len(friends))

    def ring_copy(ring, origin, number, target):
        buffer, mine, theirs, peer, send, recv = ring
        return remote(
            buffer.at[mine(origin)], buffer.at[theirs(origin, number)], send.at[number], recv.at[number], peer(target)
        )

    def ring_first(ring):
        for target in (2, -2, 1, -1):
            start(ring_copy(ring, 0, target % 8, target))

    def ring_second(ring):
        ring_wait(ring, 2)
        ring_wait(ring, 6)
        start(ring_copy(ring, None, 4, far))
        start(ring_copy(ring, -2, 3, 1))
        start(ring_copy(ring, 2, 5, -1))

    def ring_all(ring):
        for target in (4, 3, -3, 2, -2, 1, -1):
            start(ring_copy(ring, 0, target % 8, target))

    def ring_wait(ring, number):
        buffer, mine, theirs, peer, send, recv = ring
        place_of = buffer.at[theirs(-number, number)]
        remote(place_of, place_of, send.at[number], recv.at[number], peer(1)).wait_recv()

    def slot(origin):
        return SLOTS.index((origin + 3) % 8 - 3)

    def z_mine(origin):
        return slot(2) * k + slot(-2) * (1 - k) if origin is None else slot(origin)

    def z_ring(column, which):
        return (
            xg.at[k, column], z_mine, lambda origin, number: slot(-number), z_peer, az_send.at[which], az_recv.at[which]
        )

    own_ring, far_ring = z_ring(0, 0), z_ring(3, 1)

    def x_copy(column, at):
        return remote(
            xg.at[k, 0, at], xg.at[k, BACK[column], at],
            ax_send.at[column, at], ax_recv.at[BACK[column], at], x_peer(OFFSETS[column]),
        )

    def twin_copy(chunk):
        ours = xg.at[k, chunk // 2, pl.ds(chunk % 2 * blocks, blocks)]
        return remote(ours, ours, as_send.at[chunk], as_recv.at[chunk], sibling)

    def spread(origin):
        for column in (1, 2):
            start(x_copy(column, slot(origin)))

    start(x_copy(3, 0))
    ring_first(own_ring)
    spread(0)
    for load in loads[2:]:
        load.wait()
    weights = [
        remote(wgv.at[1 - k], wgs, ws_send.at[0], ws_recv.at[0], sibling),
        remote(wuv.at[1 - k], wus, ws_send.at[1], ws_recv.at[1], sibling),
        remote(wdt.at[1 - k], wds, ws_send.at[2], ws_recv.at[2], sibling),
    ]
    start(weights[0])
    start(weights[1])
    wdt[1 - k] = wdv[1 - k].T
    start(weights[2])
    wdt[k] = wdv[k].T
    for side in range(2):
        wgt[side] = wgv[side].T
        wut[side] = wuv[side].T

    def near(_):
        ring_wait(own_ring, 1)
        ring_wait(own_ring, 7)
        spread(-1)
        spread(1)
        x_copy(3, 0).wait_recv()
        ring_first(far_ring)
        ring_second(own_ring)
        spread(2)
        spread(-2)

    def rest(_):
        for number in (3, 5, 4):
            ring_wait(own_ring, number)
            spread(-number)

    def fetch(chunk):
        column, part = chunk // 2, chunk % 2
        for origin in SLOTS[part * blocks : (part + 1) * blocks]:
            if column in (1, 2):
                x_copy(BACK[column], slot(origin)).wait_recv()
            elif column == 3 and origin in (1, -1, 3, -3, 4):
                ring_wait(far_ring, -origin % 8)
        start(twin_copy(chunk))

    def pair_copy(chunk, side):
        return remote(
            sb.at[chunk, pl.ds(2 * side, 2)], (pa, pb)[side].at[chunk],
            b_send.at[chunk, side], b_recv.at[chunk, side], y_peer((1, -1)[side]),
        )

    def far_copy(chunk):
        return remote(sb.at[chunk, 4], pc.at[chunk], b_send.at[chunk, 2], b_recv.at[chunk, 2], y_peer(-far))

    def join_copy(chunk, side):
        return remote(
            sc.at[chunk, side], rc.at[chunk, side],
            b_send.at[chunk, 3 + side], b_recv.at[chunk, 3 + side], y_peer((2, -2)[side]),
        )

    def add_features(chunk):
        column, slots = chunk // 2, pl.ds(chunk % 2 * blocks, blocks)
        ours = xg[k, column, slots]
        left = ours[:, 0].reshape(rows, width)
        left_grad = ours[:, 1].reshape(rows, width)
        xo[0, chunk] = left
        xo[1, chunk] = left_grad
        sums = [
            dot(left, wgv[k], 1, 0),
            dot(left, wuv[k], 1, 0),
            dot(left_grad, wdt[k], 1, 0),
        ]
        if chunk == 0:
            for copy in weights:
                copy.wait_recv()
        twin_copy(chunk).wait_recv()
        other = xg[1 - k, column, slots]
        right = other[:, 0].reshape(rows, width)
        right_grad = other[:, 1].reshape(rows, width)
        sums[0] += dot(right, wgs[...], 1, 0)
        sums[1] += dot(right, wus[...], 1, 0)
        sums[2] += dot(right_grad, wds[...], 1, 0)
        for part in range(3):
            cols = pl.ds(part * cut, cut)
            for side in range(2):
                pf[chunk, :, pl.ds(side * share, share), cols] = sums[part][:, side * cut : (side + 1) * cut].reshape(
                    ny, share, cut
                )
        for index, step in enumerate((1, 3, -1, -3, 4)):
            sb[chunk, index] = encode(pf[chunk, along_y(step)], SUM_SCALE)
        start(far_copy(chunk))
        start(pair_copy(chunk, 0))
        start(pair_copy(chunk, 1))

    def join(chunk):
        pair_copy(chunk, 0).wait_recv()
        pair_copy(chunk, 1).wait_recv()
        far_copy(chunk).wait_recv()
        distant = decode(pc[chunk], SUM_SCALE)
        second = k.astype(jnp.float32)
        ahead = pf[chunk, along_y(2)] + decode(pa[chunk, 1], SUM_SCALE) + distant * second
        behind = pf[chunk, along_y(-2)] + decode(pb[chunk, 1], SUM_SCALE) + distant * (1.0 - second)
        sc[chunk, 0] = encode(ahead, SUM_SCALE)
        sc[chunk, 1] = encode(behind, SUM_SCALE)
        start(join_copy(chunk, 0))
        start(join_copy(chunk, 1))

    def y_ring(chunk):
        def mine(origin):
            return along_y(-far if origin is None else origin)

        return (hb.at[chunk, k], mine, lambda origin, _: mine(origin), y_peer, c_send.at[chunk], c_recv.at[chunk])

    def half_copy(chunk):
        ours = hb.at[chunk, k]
        return remote(ours, ours, cs_send.at[chunk], cs_recv.at[chunk], sibling)

    def gate(chunk):
        join_copy(chunk, 0).wait_recv()
        join_copy(chunk, 1).wait_recv()
        total = pf[chunk, y] + decode(pa[chunk, 0], SUM_SCALE) + decode(pb[chunk, 0], SUM_SCALE)
        total += decode(rc[chunk, 0], SUM_SCALE) + decode(rc[chunk, 1], SUM_SCALE)
        gate_pre = total[:, :cut]
        up_pre = total[:, cut : 2 * cut]
        hidden_delta = total[:, 2 * cut :]
        sigma = jax.nn.sigmoid(gate_pre)
        silu_gate = gate_pre * sigma
        slope = sigma * (1.0 + gate_pre * (1.0 - sigma))
        hb[chunk, k, y, 0] = (silu_gate * up_pre).astype(jnp.bfloat16)
        hb[chunk, k, y, 1] = (hidden_delta * up_pre * slope).astype(jnp.bfloat16)
        hb[chunk, k, y, 2] = (hidden_delta * silu_gate).astype(jnp.bfloat16)
        if chunk == LAST:
            ring_all(y_ring(chunk))
        else:
            ring_first(y_ring(chunk))

    def block_copy(column, chunk, index):
        step = SLOTS[index] % nz
        return remote(
            ib.at[chunk, index % blocks], jb.at[BACK[column], step],
            dx_send.at[column, step], dx_recv.at[BACK[column], step], plane_peer(step, OFFSETS[column]),
        )

    def term(chunk, side):
        for array in range(3):
            pieces = hb[chunk, side, :, array].astype(jnp.float32)
            first = pieces[:, :share].reshape(rows, cut)
            second = pieces[:, share:].reshape(rows, cut)
            ho[array, side, chunk] = jnp.concatenate([first, second], axis=1).astype(jnp.bfloat16)
        return dot(ho[1, side, chunk], wgt[side], 1, 0) + dot(ho[2, side, chunk], wut[side], 1, 0)

    def share_half(chunk):
        for number in (1, 7, 2, 6, 3, 5, 4) if chunk == LAST else (1, 7, 3, 5, 4):
            ring_wait(y_ring(chunk), number)
        start(half_copy(chunk))

    def grad(chunk):
        total = term(chunk, k)
        half_copy(chunk).wait_recv()
        total = (total + term(chunk, 1 - k)).reshape(blocks, block, width)
        if chunk == 1:
            tail[...] = total
            return
        ib[chunk] = encode(total, GRAD_SCALE)
        if chunk == 0:
            own[...] = total[0]
        if chunk in (3, 5):
            start(column_copy(chunk // 2))
        else:
            send_blocks(chunk)

    def send_blocks(chunk):
        column, part = chunk // 2, chunk % 2
        for index in reversed(range(part * blocks, (part + 1) * blocks)):
            if column or index:
                start(block_copy(column, chunk, index))

    def column_copy(column):
        return remote(
            ib.at[2 * column + 1], mb.at[BACK[column] - 1],
            mx_send.at[column - 1], mx_recv.at[BACK[column] - 1], x_peer(OFFSETS[column]),
        )

    def merge(chunk):
        total = tail[...]
        for column in (1, 2):
            column_copy(BACK[column]).wait_recv()
            total += decode(mb[column - 1], GRAD_SCALE)
        ib[chunk] = encode(total, GRAD_SCALE)
        send_blocks(chunk)

    actions = {
        "near": near, "far": lambda _: ring_second(far_ring), "rest": rest,
        "fetch": fetch, "sum": add_features, "join": join, "gate": gate,
        "pass": lambda chunk: ring_second(y_ring(chunk)), "half": share_half, "grad": grad,
        "merge": merge,
    }
    for step in STEPS:
        actions[step[:-1]](int(step[-1]))

    tokens = 2 * nx * rows
    left = xo[0].reshape(tokens, width)
    for side in range(2):
        cols = pl.ds(side * half, half)
        ggv[:, cols] = dot(left, ho[1, side].reshape(tokens, half), 0, 0).astype(jnp.bfloat16)
        ugv[:, cols] = dot(left, ho[2, side].reshape(tokens, half), 0, 0).astype(jnp.bfloat16)
    stores = [
        pltpu.make_async_copy(ggv, gg_out, load_sem.at[0]),
        pltpu.make_async_copy(ugv, ug_out, load_sem.at[1]),
        pltpu.make_async_copy(dgv, dg_out, load_sem.at[2]),
        pltpu.make_async_copy(igv, ig_out, load_sem.at[3]),
    ]
    stores[0].start()
    stores[1].start()
    right = xo[1].reshape(tokens, width)
    for side in range(2):
        cols = pl.ds(side * half, half)
        dgv[cols] = dot(ho[0, side].reshape(tokens, half), right, 0, 0).astype(jnp.bfloat16)
    stores[2].start()

    for copy in sent:
        copy.wait_send()
    total = own[...]
    for column in (1, 2, 3, 0):
        for index in range(nz if column in (0, 3) else blocks):
            if column or index:
                block_copy(BACK[column], 0, index).wait_recv()
                total += decode(jb[column, SLOTS[index] % nz], GRAD_SCALE)
    igv[...] = total.astype(jnp.bfloat16)
    stores[3].start()
    for store in stores:
        store.wait()


def hand_over(*refs):
    count = len(refs) // 3
    given, out, held, sems = refs[:count], refs[count : 2 * count], refs[2 * count : 3 * count], refs[-1]
    loads = [pltpu.make_async_copy(given[i], held[i], sems.at[0, i]) for i in range(count)]
    stores = [pltpu.make_async_copy(held[i], out[i], sems.at[1, i]) for i in range(count)]
    for load in loads:
        load.start()
    for load, store in zip(loads, stores):
        load.wait()
        store.start()
    for store in stores:
        store.wait()


def shards(ny, nz, tokens, grad_output, gate_weight, up_weight, down_weight):
    block, width = tokens.shape
    hidden = gate_weight.shape[1] // 2
    half = hidden // 2
    nx = 4
    chunks, rows, cut = 2 * nx, nz // 2 * block, half // 2
    bf16, f32 = jnp.bfloat16, jnp.float32
    vmem, dma = pltpu.VMEM, pltpu.SemaphoreType.DMA
    results = (
        jax.ShapeDtypeStruct((block, width), bf16),
        jax.ShapeDtypeStruct((width, hidden), bf16),
        jax.ShapeDtypeStruct((width, hidden), bf16),
        jax.ShapeDtypeStruct((hidden, width), bf16),
    )
    made = pl.pallas_call(
        functools.partial(kernel, ny, nz),
        out_shape=results,
        in_specs=[pl.BlockSpec(memory_space=pl.ANY)] * 5,
        out_specs=[pl.BlockSpec(memory_space=pl.ANY)] * 4,
        scratch_shapes=[
            vmem((2, nx, nz, 2, block, width), bf16),
            vmem((2, width, half), bf16),
            vmem((2, width, half), bf16),
            vmem((2, half, width), bf16),
            vmem((width, half), bf16),
            vmem((width, half), bf16),
            vmem((width, half), bf16),
            vmem((2, half, width), bf16),
            vmem((2, half, width), bf16),
            vmem((2, width, half), bf16),
            vmem((2, chunks, rows, width), bf16),
            vmem((chunks, ny, block, 3 * cut), f32),
            vmem((chunks, 5, block, 3 * cut), bf16),
            vmem((chunks, 2, block, 3 * cut), bf16),
            vmem((chunks, 2, block, 3 * cut), bf16),
            vmem((chunks, block, 3 * cut), bf16),
            vmem((chunks, 2, block, 3 * cut), bf16),
            vmem((chunks, 2, block, 3 * cut), bf16),
            vmem((chunks, 2, ny, 3, block, cut), bf16),
            vmem((3, 2, chunks, rows, half), bf16),
            vmem((block, width), f32),
            vmem((chunks, nz // 2, block, width), bf16),
            vmem((nx, nz, block, width), bf16),
            vmem((2, nz // 2, block, width), bf16),
            vmem((nz // 2, block, width), f32),
            vmem((width, hidden), bf16),
            vmem((width, hidden), bf16),
            vmem((hidden, width), bf16),
            vmem((block, width), bf16),
            dma((8,)),
            dma((2, nz)), dma((2, nz)),
            dma((nx, nz)), dma((nx, nz)),
            dma((chunks,)), dma((chunks,)),
            dma((3,)), dma((3,)),
            dma((chunks, 5)), dma((chunks, 5)),
            dma((chunks, ny)), dma((chunks, ny)),
            dma((chunks,)), dma((chunks,)),
            dma((nx, nz)), dma((nx, nz)),
            dma((2,)), dma((2,)),
        ],
        compiler_params=pltpu.CompilerParams(
            collective_id=0, has_side_effects=True, vmem_limit_bytes=60 * 2**20
        ),
        name="ffn_backward",
    )(tokens, grad_output, gate_weight, up_weight, down_weight)
    return pl.pallas_call(
        hand_over,
        out_shape=results,
        in_specs=[pl.BlockSpec(memory_space=pl.ANY)] * 4,
        out_specs=[pl.BlockSpec(memory_space=pl.ANY)] * 4,
        scratch_shapes=[vmem(result.shape, bf16) for result in results] + [dma((2, 4))],
        compiler_params=pltpu.CompilerParams(vmem_limit_bytes=60 * 2**20),
        name="hand_over",
    )(*made)


def solution(mesh):
    placed = (
        P(("col", "depth"), "row"),
        P(("col", "depth"), "row"),
        P("row", "col"),
        P("row", "col"),
        P("col", "row"),
    )
    ny, nz = mesh.shape["row"] // 2, mesh.shape["col"] // 2
    return jax.shard_map(
        functools.partial(shards, ny, nz),
        mesh=mesh,
        in_specs=placed,
        out_specs=(
            P(("col", "depth"), "row"),
            P("row", ("col", "depth")),
            P("row", ("col", "depth")),
            P(("col", "depth"), "row"),
        ),
        check_vma=False,
    )
```
